32 devices in a mesh: groups: 2 (over y), zone: 4 (over z), scen: 2 (over x), hour: 2 (over core).
Axes of the slice: x: 2, y: 2, z: 4, core: 2. Of those that a mesh axis runs over, the one named last changes fastest.
Arguments:
- forcing: bfloat16 [1024, 48, 64], P(('groups', 'zone', 'scen', 'hour')), parts along dimension 0, may hold values from -3 to 3
- response: bfloat16 [48, 64, 8192], P('hour', None, ('groups', 'zone')), parts along dimension 2, may hold values from -0.75 to 0.75
- window_params: float32 [128, 64], P('groups'), parts along dimension 0, may hold values from 0.5 to 1.5
- building_map: int32 [8192], P(('groups', 'zone')), parts along dimension 0, may hold values from 0 to 1023
- owner_ids: int32 [2048], P('groups'), parts along dimension 0, may hold values from 0 to 63
- band_ids: int32 [48, 8192], P('hour', ('groups', 'zone')), parts along dimension 1, may hold values from 0 to 7
- floor_area: float32 [8192], P(('groups', 'zone')), parts along dimension 0, may hold values from 0.5 to 18, as said below
Outputs:
- sensitivity: float32 [128, 64], P(('groups', 'zone', 'scen', 'hour')), parts along dimension 0
- objective: float32 [2], P('groups'), parts along dimension 0
The draws below stay inside these ranges and needn't reach their ends.
There are 2 independent parts, one for each index of `groups`. The reference program is written for one: setup_inputs(seed, part) draws one part's arguments, and reference() takes and returns one part's arrays. A program takes and returns all parts, laid end to end along the dimension named above; each array names one. Nothing has to cross between parts.
Inputs may be any that keep to these rules, and one draw needn't show every extreme that they name: `floor_area`: floor areas are positive.
All inputs are finite; a program needn't handle non-finite values.
Results may differ from the reference program's by a relative error of at most 0.0006.
Values may be sent and summed in bfloat16 or wider, within the bound.
A program may use at most 128 MiB of HBM per device.

```python
import math
import jax
import jax.numpy as jnp
from jax import lax

WINDOW_COUNT = 64
BANDS = 8
HOURS = 48
SCENARIOS = 512
ZONES = 4096
DESIGNS = 64
BUILDINGS = 1024


def draw_floor_area(key, part):
    position = jnp.arange(ZONES).astype(jnp.float32) / (ZONES - 1)
    trend = jnp.exp(math.log(3.0) * position)
    noise = jnp.exp(jax.random.uniform(key, (ZONES,), jnp.float32, math.log(0.5), math.log(2.0)))
    return (trend * noise).astype(jnp.float32)


def set_ends(drawn, key, low, largest):
    longest = drawn.shape.index(max(drawn.shape))
    spots = []
    for shift in (0, 1):
        where = [jax.random.randint(jax.random.fold_in(key, axis), (), 0, length) for axis, length in enumerate(drawn.shape)]
        where[longest] = (where[longest] + shift) % drawn.shape[longest]
        spots.append(tuple(where))
    return drawn.at[spots[0]].set(low).at[spots[1]].set(largest)


def block_levels(own_key, extent, pieces, low, top_value):
    factor_of = 1.0
    for dim, blocks in pieces:
        heights = jax.random.uniform(jax.random.fold_in(jax.random.fold_in(own_key, 6), dim), (blocks,), jnp.float32, low / len(pieces), top_value / len(pieces))
        factor_of = factor_of * jnp.repeat(jnp.exp(heights), extent[dim] // blocks).reshape((-1,) + (1,) * (len(extent) - 1 - dim))
    return factor_of


def gaussian(key, shape, deviation, bound, shards=(), kind=jnp.bfloat16):
    array = deviation * jax.random.normal(key, shape, jnp.float32)
    if shards:
        array = array * block_levels(key, shape, shards, -0.22, 0.18)
    return jnp.clip(array, -bound, bound).astype(kind)


def setup_inputs(seed: int = 0, part: int = 0) -> dict:
    seeds = jax.random.split(jax.random.key(seed), 8)
    own_keys = jax.random.split(jax.random.fold_in(seeds[7], part), 8)
    forcing = gaussian(own_keys[0], (SCENARIOS, HOURS, WINDOW_COUNT), 0.5, 3.0, ((0, 16),))
    response = gaussian(own_keys[1], (HOURS, WINDOW_COUNT, ZONES), WINDOW_COUNT ** -0.5, 0.75, ((0, 2), (2, 4)))
    window_params = jnp.clip(jax.random.uniform(own_keys[2], (DESIGNS, WINDOW_COUNT), jnp.float32, 0.5, 1.5), 0.5, 1.5)
    building_map = set_ends(jax.random.randint(own_keys[3], (ZONES,), 0, BUILDINGS), jax.random.fold_in(own_keys[3], 1), 0, BUILDINGS - 1).astype(jnp.int32)
    owner_ids = set_ends(jax.random.randint(own_keys[4], (BUILDINGS,), 0, DESIGNS), jax.random.fold_in(own_keys[4], 1), 0, DESIGNS - 1).astype(jnp.int32)
    band_ids = set_ends(jax.random.randint(own_keys[5], (HOURS, ZONES), 0, BANDS), jax.random.fold_in(own_keys[5], 1), 0, BANDS - 1).astype(jnp.int32)
    floor_area = draw_floor_area(jax.random.fold_in(jax.random.fold_in(seeds[7], part), 71), part)
    return dict(forcing=forcing, response=response, window_params=window_params, building_map=building_map, owner_ids=owner_ids, band_ids=band_ids, floor_area=floor_area)


SHARPNESS = 200.0

def reference(forcing, response, window_params, building_map, owner_ids, band_ids, floor_area):
    candidate_plan = owner_ids[building_map].astype(jnp.int32)
    zone_parameters = window_params[candidate_plan]
    lower_factor = lax.optimization_barrier((response.astype(jnp.float32) * zone_parameters.T[None, :, :]).astype(jnp.bfloat16))
    coeff_full = lower_factor.astype(jnp.float32)
    positions = jnp.arange(HOURS).astype(jnp.float32)
    occupant_level = 1.0 + 2.0 * positions / (HOURS - 1)
    zone_weight = occupant_level[:, None] * floor_area[None, :]
    weight_total = jnp.sum(floor_area) * jnp.sum(occupant_level)
    band_low = 0.25 * (band_ids.astype(jnp.float32) - 3.5) - 0.5
    band_high = band_low + 1.0
    blocks = forcing.reshape(SCENARIOS // 16, 16, HOURS, WINDOW_COUNT)
    response_full = response.astype(jnp.float32)

    def heat_of(record_elements):
        return jnp.einsum('shp,hpz->shz', record_elements.astype(jnp.float32), coeff_full)

    def loss_block(record_elements):
        thermal_demand = heat_of(record_elements)
        penalty = jax.nn.softplus(thermal_demand - band_high[None]) + jax.nn.softplus(band_low[None] - thermal_demand)
        return lax.optimization_barrier(jnp.sum(penalty * zone_weight[None], axis=(1, 2)))
    losses = lax.map(loss_block, blocks).reshape(SCENARIOS)
    scores = SHARPNESS * losses / weight_total
    peak_score = jnp.max(scores)
    exp_total = jnp.sum(jnp.exp(scores - peak_score))
    objective = ((peak_score + jnp.log(exp_total)) / SHARPNESS).reshape(1)
    scen_weight = jnp.exp(scores - peak_score) / exp_total / weight_total

    def grad_step(accumulated, inputs):
        record_elements, row_weight = inputs
        thermal_demand = heat_of(record_elements)
        slope = jax.nn.sigmoid(thermal_demand - band_high[None]) - jax.nn.sigmoid(band_low[None] - thermal_demand)
        adjoint = slope * row_weight[:, None, None] * zone_weight[None]
        adjoint = lax.optimization_barrier(adjoint.astype(jnp.bfloat16)).astype(jnp.float32)
        mixed = jnp.einsum('shp,shz->hpz', record_elements.astype(jnp.float32), adjoint)
        return (accumulated + lax.optimization_barrier(jnp.sum(response_full * mixed, axis=0)), None)
    zone_grad, unused = lax.scan(grad_step, jnp.zeros((WINDOW_COUNT, ZONES), jnp.float32), (blocks, scen_weight.reshape(SCENARIOS // 16, 16)))
    gain = math.sqrt(WINDOW_COUNT * ZONES * HOURS * DESIGNS)
    sensitivity = jax.ops.segment_sum(zone_grad.T, candidate_plan, num_segments=DESIGNS) * gain
    return (sensitivity, objective)
```

```python
import functools
import math

import jax
import jax.numpy as jnp
from jax import lax
from jax.experimental import pallas as pl
from jax.experimental.pallas import tpu as pltpu
from jax.sharding import PartitionSpec as P

SHARPNESS = 200.0
LOG2E = 1.4426950408889634
LN2 = 0.6931471805599453
CROSS = 2.0 * math.cosh(0.5)
HIGH = lax.Precision.HIGHEST
MESH = pl.DeviceIdType.MESH
TN = (((0,), (0,)), ((), ()))
NT = (((1,), (1,)), ((), ()))


def split3(x):
    hi = x.astype(jnp.bfloat16)
    rest = x - hi.astype(jnp.float32)
    mid = rest.astype(jnp.bfloat16)
    lo = (rest - mid.astype(jnp.float32)).astype(jnp.bfloat16)
    return hi, mid, lo


def kernel(
    zn, sn, hn, gathered, hours_total,
    fx_ref, resp_hbm, wp_ref, map_ref, own_ref, band_ref, floor_ref,
    sens_ref, obj_ref,
    f_all, resp, ft, slope, prm, plan, wcol, acc, zg, sums, parts, rbuf,
    resp_sem, own_sem, fsend, frecv, ssend, srecv, rsend, rrecv,
):
    n = zn * sn * hn
    my_z = lax.axis_index("zone")
    my_s = lax.axis_index("scen")
    my_h = lax.axis_index("hour")
    me = (my_z * sn + my_s) * hn + my_h
    hours, width, zones = resp.shape
    chunks, slots, per, rows, lanes = f_all.shape
    scens = slots * rows

    resp_copy = pltpu.make_async_copy(resp_hbm, resp, resp_sem)
    resp_copy.start()

    def at(i):
        return {"zone": i // (sn * hn), "scen": (i // hn) % sn, "hour": i % hn}

    barrier = pltpu.get_barrier_semaphore()

    def greet(k, c):
        pl.semaphore_signal(barrier, inc=1, device_id=at((me + k) % n), device_id_type=MESH)
        return c

    lax.fori_loop(1, n, greet, 0)
    pl.semaphore_wait(barrier, n - 1)

    mine = my_z * hn + my_h

    def feed(c, k):
        peer = (mine + k) % slots
        pz, ph = peer // hn, peer % hn
        return pltpu.make_async_remote_copy(
            src_ref=fx_ref.at[ph * chunks + c],
            dst_ref=f_all.at[c, mine],
            send_sem=fsend.at[c, k],
            recv_sem=frecv.at[c, k],
            device_id={"zone": pz, "hour": ph},
            device_id_type=MESH,
        )

    if gathered:
        own_copies = []
        for c in range(chunks):
            own_copies.append(pltpu.make_async_copy(fx_ref.at[c], f_all.at[c, 0], own_sem.at[c]))
            own_copies[-1].start()
    else:
        own_copies = []
        for c in range(chunks):
            cp = pltpu.make_async_copy(fx_ref.at[my_h * chunks + c], f_all.at[c, mine], own_sem.at[c])
            cp.start()
            own_copies.append(cp)
            for k in range(1, slots):
                feed(c, k).start()

    buildings = own_ref.shape[1]
    bstep = min(buildings, 1024)
    zmap = map_ref[...]
    row16 = lax.broadcasted_iota(jnp.int32, (16, bstep), 0)

    def find(i, total):
        start = pl.multiple_of(i * bstep, bstep)
        own = own_ref[:, pl.ds(start, bstep)]
        high = own // 128
        digits = jnp.where(row16 == 0, high, jnp.where(row16 == 1, own - high * 128, 0))
        digits = digits.astype(jnp.float32).astype(jnp.bfloat16)
        ids = lax.broadcasted_iota(jnp.int32, (bstep, zones), 0) + start
        hot = (ids == zmap).astype(jnp.float32).astype(jnp.bfloat16)
        return total + jnp.dot(digits, hot, preferred_element_type=jnp.float32)

    found = lax.fori_loop(0, buildings // bstep, find, jnp.zeros((16, zones), jnp.float32))
    owner = found[0:1, :] * 128.0 + found[1:2, :]
    plan[...] = owner.astype(jnp.int32)

    designs = wp_ref.shape[0]
    dstep = min(designs, 64)

    def pick(i, total):
        start = pl.multiple_of(i * dstep, dstep)
        ids = lax.broadcasted_iota(jnp.int32, (dstep, zones), 0) + start
        hot = (ids == plan[...]).astype(jnp.float32).astype(jnp.bfloat16)
        for piece in split3(wp_ref[pl.ds(start, dstep), :]):
            total = total + lax.dot_general(piece, hot, TN, preferred_element_type=jnp.float32)
        return total

    prm[...] = lax.fori_loop(0, designs // dstep, pick, jnp.zeros((width, zones), jnp.float32))

    acc[...] = jnp.zeros_like(acc)
    lane = lax.broadcasted_iota(jnp.int32, (scens, lanes), 1)
    pad_row = lax.broadcasted_iota(jnp.int32, (width, zones), 0)
    hour_first = my_h * hours

    def occupancy(h):
        position = (hour_first + h).astype(jnp.float32)
        return 1.0 + 2.0 * position / (hours_total - 1)

    resp_copy.wait()
    row_tile, zone_tile = min(64, scens), 256

    for c in range(chunks):
        own_copies[c].wait()
        if not gathered:
            for k in range(1, slots):
                feed(c, k).wait()

        def pair_body(k, carry):
            j = c * per + k
            f2 = f_all[c, :, pl.ds(k, 1), :, :].reshape(scens, lanes)
            ft[j] = f2.astype(jnp.float32).T
            for half in range(2):
                h = 2 * j + half
                coeff = (resp[h].astype(jnp.float32) * prm[...]).astype(jnp.bfloat16)
                mid = 0.25 * (band_ref[pl.ds(h, 1), :].astype(jnp.float32) - 3.5)
                pad = jnp.where(pad_row == 0, -mid, 0.0).astype(jnp.bfloat16)
                if half == 0:
                    left = jnp.where(lane < width, f2.astype(jnp.float32), jnp.where(lane == width, 1.0, 0.0))
                    wcol[half] = jnp.concatenate([coeff, pad], axis=0)
                else:
                    left = jnp.where(lane >= width, f2.astype(jnp.float32), jnp.where(lane == 0, 1.0, 0.0))
                    wcol[half] = jnp.concatenate([pad, coeff], axis=0)
                left = left.astype(jnp.bfloat16)
                weight = floor_ref[...] * occupancy(h)
                for zt in range(zones // zone_tile):
                    zs = slice(zt * zone_tile, (zt + 1) * zone_tile)
                    w_tile = weight[:, zs]
                    for st in range(scens // row_tile):
                        ss = slice(st * row_tile, (st + 1) * row_tile)
                        u = jnp.dot(left[ss, :], wcol[half, :, zs], preferred_element_type=jnp.float32)
                        a = jnp.abs(u) * (-LOG2E)
                        t = jnp.exp2(a)
                        q = t * (t + CROSS) + 1.0
                        cost = (jnp.log2(q) - a) * w_tile
                        part = cost[:, 0:128]
                        for i in range(1, zone_tile // 128):
                            part = part + cost[:, i * 128:(i + 1) * 128]
                        acc[ss, :] += part
                        ub = (u * 0.5).astype(jnp.bfloat16)
                        slope[h, ss, zs] = jnp.tanh(ub - 0.25) + jnp.tanh(ub + 0.25)
            return carry

        lax.fori_loop(0, per, pair_body, 0)

    ones = jnp.ones((8, 128), jnp.float32)
    mysum = lax.dot_general(ones, acc[...], NT, precision=HIGH, preferred_element_type=jnp.float32)[0:1, :]
    floor_sum = jnp.sum(floor_ref[...], axis=1, keepdims=True)
    occ_sum = hours + 2.0 / (hours_total - 1) * (
        hours * hour_first.astype(jnp.float32) + hours * (hours - 1) / 2.0
    )
    mw = floor_sum * occ_sum
    mysum = (mysum * LN2) - 0.5 * mw
    slot = my_z * hn + my_h
    sums[my_s, slot] = jnp.concatenate([mysum, jnp.broadcast_to(mw, (1, 128))], axis=1)

    def tell(k):
        return pltpu.make_async_remote_copy(
            src_ref=sums.at[my_s, slot],
            dst_ref=sums.at[my_s, slot],
            send_sem=ssend.at[k],
            recv_sem=srecv.at[k],
            device_id=at((me + k) % n),
            device_id_type=MESH,
        )

    def tell_start(k, c):
        tell(k).start()
        return c

    def heard(k):
        peer = (me + n - k) % n
        ref = sums.at[(peer // hn) % sn, (peer // (sn * hn)) * hn + peer % hn]
        return pltpu.make_async_remote_copy(
            src_ref=ref, dst_ref=ref, send_sem=ssend.at[k], recv_sem=srecv.at[k],
            device_id=at((me + k) % n), device_id_type=MESH,
        )

    def tell_wait(k, c):
        heard(k).wait_recv()
        return c

    def tell_sent(k, c):
        tell(k).wait_send()
        return c

    lax.fori_loop(1, n, tell_start, 0)
    lax.fori_loop(1, n, tell_wait, 0)

    totals = [jnp.sum(sums[s], axis=0) for s in range(sn)]
    wt = totals[0][:, scens:scens + 1]
    scores = [SHARPNESS * t[:, :scens] / wt for t in totals]
    peak = jnp.max(scores[0], axis=1, keepdims=True)
    for s in scores[1:]:
        peak = jnp.maximum(peak, jnp.max(s, axis=1, keepdims=True))
    exp_total = jnp.sum(jnp.exp(scores[0] - peak), axis=1, keepdims=True)
    for s in scores[1:]:
        exp_total = exp_total + jnp.sum(jnp.exp(s - peak), axis=1, keepdims=True)
    obj_ref[...] = jnp.broadcast_to((peak + jnp.log(exp_total)) / SHARPNESS, obj_ref.shape)
    my_total = jnp.sum(sums[my_s], axis=0)
    sw = jnp.exp(SHARPNESS * my_total[:, :scens] / wt - peak) / exp_total
    lax.fori_loop(1, n, tell_sent, 0)

    zg[...] = jnp.zeros_like(zg)

    def mix_body(j, carry):
        for half in range(2):
            h = 2 * j + half
            fw = ft[j, half * width:(half + 1) * width, :] * (sw * occupancy(h))
            hi = fw.astype(jnp.bfloat16)
            lo = (fw - hi.astype(jnp.float32)).astype(jnp.bfloat16)
            both = jnp.concatenate([hi, lo], axis=0)
            mixed = jnp.dot(both, slope[h], preferred_element_type=jnp.float32)
            zg[...] += resp[h].astype(jnp.float32) * (mixed[:width] + mixed[width:])
        return carry

    lax.fori_loop(0, hours // 2, mix_body, 0)

    zones_all = zones * zn
    gain = 0.5 * math.sqrt(width * zones_all * hours_total * designs)
    pieces = split3(zg[...] * floor_ref[...] * (gain / wt))
    each = designs // n
    block = 8 * min(n, 16)

    def own_body(i, carry):
        r = lax.broadcasted_iota(jnp.int32, (block, zones), 0) + i * block
        ids = jnp.where(r % 8 < each, (r // 8) * each + r % 8, -1)
        hot = (ids == plan[...]).astype(jnp.float32).astype(jnp.bfloat16)
        total = jnp.zeros((block, width), jnp.float32)
        for piece in pieces:
            total = total + lax.dot_general(hot, piece, NT, preferred_element_type=jnp.float32)
        for b in range(block // 8):
            parts[i * (block // 8) + b] = total[b * 8:(b + 1) * 8, :]
        return carry

    lax.fori_loop(0, n // (block // 8), own_body, 0)

    def give(k):
        peer = (me + k) % n
        return pltpu.make_async_remote_copy(
            src_ref=parts.at[peer],
            dst_ref=rbuf.at[k],
            send_sem=rsend.at[k],
            recv_sem=rrecv.at[k],
            device_id=at(peer),
            device_id_type=MESH,
        )

    def give_start(k, c):
        give(k).start()
        return c

    def give_wait(k, c):
        give(k).wait()
        return c

    lax.fori_loop(1, n, give_start, 0)
    rbuf[0] = parts[me]
    lax.fori_loop(1, n, give_wait, 0)
    sens_ref[...] = jnp.sum(rbuf[...], axis=0)[:each, :]


def on_device(forcing, response, window_params, building_map, owner_ids, band_ids, floor_area):
    zn, sn, hn = lax.axis_size("zone"), lax.axis_size("scen"), lax.axis_size("hour")
    n = zn * sn * hn
    hours, width, zones = response.shape
    rows = forcing.shape[0]
    pairs = hours // 2
    gathered = rows % 16 != 0
    if gathered:
        chunks, slots, rows_in = 1, 1, rows * zn * hn
        mine = lax.all_to_all(forcing, "hour", split_axis=1, concat_axis=0, tiled=True)
        whole = lax.all_gather(mine, "zone", axis=0, tiled=True)
        fx = whole.reshape(rows_in, pairs, 2 * width).transpose(1, 0, 2)[None]
    else:
        chunks, slots, rows_in = 4, zn * hn, rows
        fx = forcing.reshape(rows, hn * pairs, 2 * width).transpose(1, 0, 2)
        fx = fx.reshape(hn * chunks, pairs // chunks, rows, 2 * width)
    per = pairs // chunks
    scens = slots * rows_in
    designs = window_params.shape[0]
    vm = pl.BlockSpec(memory_space=pltpu.VMEM)
    anyspace = pl.BlockSpec(memory_space=pl.ANY)
    dma = pltpu.SemaphoreType.DMA
    f32, bf16 = jnp.float32, jnp.bfloat16
    sens, obj = pl.pallas_call(
        functools.partial(kernel, zn, sn, hn, gathered, hours * hn),
        out_shape=(
            jax.ShapeDtypeStruct((designs // n, width), f32),
            jax.ShapeDtypeStruct((1, 128), f32),
        ),
        in_specs=[anyspace, anyspace, vm, vm, vm, vm, vm],
        out_specs=(vm, vm),
        scratch_shapes=[
            pltpu.VMEM((chunks, slots, per, rows_in, 2 * width), bf16),
            pltpu.VMEM((hours, width, zones), bf16),
            pltpu.VMEM((pairs, 2 * width, scens), f32),
            pltpu.VMEM((hours, scens, zones), bf16),
            pltpu.VMEM((width, zones), f32),
            pltpu.VMEM((1, zones), jnp.int32),
            pltpu.VMEM((2, 2 * width, zones), bf16),
            pltpu.VMEM((scens, 128), f32),
            pltpu.VMEM((width, zones), f32),
            pltpu.VMEM((sn, zn * hn, 1, scens + 128), f32),
            pltpu.VMEM((n, 8, width), f32),
            pltpu.VMEM((n, 8, width), f32),
            dma,
            dma((chunks,)),
            dma((chunks, slots)),
            dma((chunks, slots)),
            dma((n,)),
            dma((n,)),
            dma((n,)),
            dma((n,)),
        ],
        compiler_params=pltpu.CompilerParams(
            collective_id=0, has_side_effects=True, vmem_limit_bytes=56 * 1024 * 1024
        ),
        cost_estimate=pl.CostEstimate(
            flops=6 * scens * hours * width * zones,
            bytes_accessed=2 * hours * width * zones,
            transcendentals=4 * scens * hours * zones,
        ),
    )(
        fx, response, window_params, building_map.reshape(1, -1), owner_ids.reshape(1, -1),
        band_ids, floor_area.reshape(1, -1),
    )
    return (sens, obj[0, :1])


def solution(mesh):
    in_specs = (
        P(("groups", "zone", "scen", "hour"), None, None),
        P("hour", None, ("groups", "zone")),
        P("groups", None),
        P(("groups", "zone")),
        P("groups"),
        P("hour", ("groups", "zone")),
        P(("groups", "zone")),
    )
    out_specs = (P(("groups", "zone", "scen", "hour"), None), P("groups"))
    return jax.shard_map(
        on_device, mesh=mesh, in_specs=in_specs, out_specs=out_specs, check_vma=False
    )
```

```python
import functools
import math

import jax
import jax.numpy as jnp
from jax import lax
from jax.experimental import pallas as pl
from jax.experimental.pallas import tpu as pltpu
from jax.sharding import PartitionSpec as P

SHARPNESS = 200.0
LOG2E = 1.4426950408889634
LN2 = 0.6931471805599453
CROSS = 2.0 * math.cosh(0.5)
HIGH = lax.Precision.HIGHEST
MESH = pl.DeviceIdType.MESH
AHEAD = 2
TN = (((0,), (0,)), ((), ()))
NT = (((1,), (1,)), ((), ()))


def split3(x):
    hi = x.astype(jnp.bfloat16)
    rest = x - hi.astype(jnp.float32)
    mid = rest.astype(jnp.bfloat16)
    lo = (rest - mid.astype(jnp.float32)).astype(jnp.bfloat16)
    return hi, mid, lo


def chunk_cuts(pairs):
    sizes = [2] * (pairs // 2) + [1] * (pairs % 2)
    return [(sum(sizes[:i]), size) for i, size in enumerate(sizes)]


def kernel(
    zn, sn, hn, gathered, hours_total,
    fx_ref, resp_hbm, wp_ref, map_ref, own_ref, band_ref, floor_ref,
    sens_ref, obj_ref,
    f_all, resp, ft, slope, prm, plan, wcol, acc, zg, sums, parts, rbuf,
    resp_sem, own_sem, fsend, frecv, ssend, srecv, rsend, rrecv,
):
    n = zn * sn * hn
    my_z = lax.axis_index("zone")
    my_s = lax.axis_index("scen")
    my_h = lax.axis_index("hour")
    me = (my_z * sn + my_s) * hn + my_h
    hours, width, zones = resp.shape
    pairs, slots, rows, lanes = f_all.shape
    cuts = chunk_cuts(pairs)
    scens = slots * rows

    resp_copy = pltpu.make_async_copy(resp_hbm, resp, resp_sem)
    resp_copy.start()

    def each_peer(body):
        if n <= 32:
            for k in range(1, n):
                body(k)
        else:
            lax.fori_loop(1, n, lambda k, c: (body(k), c)[1], 0)

    def away(k, sign=1):
        dz, ds, dh = k // (sn * hn), (k // hn) % sn, k % hn
        if sign < 0:
            dz, ds, dh = zn - dz, sn - ds, hn - dh
        return (my_z + dz) % zn, (my_s + ds) % sn, (my_h + dh) % hn

    def at(k):
        z, s, h = away(k)
        return {"zone": z, "scen": s, "hour": h}

    barrier = pltpu.get_barrier_semaphore()

    def greet(k):
        pl.semaphore_signal(barrier, inc=1, device_id=at(k), device_id_type=MESH)

    each_peer(greet)
    pl.semaphore_wait(barrier, n - 1)

    mine = my_z * hn + my_h

    def feed(c, k):
        first, count = cuts[c]
        pz, ph = (my_z + k // hn) % zn, (my_h + k % hn) % hn
        return pltpu.make_async_remote_copy(
            src_ref=fx_ref.at[pl.ds(ph * pairs + first, count)],
            dst_ref=f_all.at[pl.ds(first, count), mine],
            send_sem=fsend.at[c, k],
            recv_sem=frecv.at[c, k],
            device_id={"zone": pz, "hour": ph},
            device_id_type=MESH,
        )

    own_copies = []
    for c, (first, count) in enumerate(cuts):
        start = first if gathered else my_h * pairs + first
        cp = pltpu.make_async_copy(
            fx_ref.at[pl.ds(start, count)],
            f_all.at[pl.ds(first, count), 0 if gathered else mine],
            own_sem.at[c],
        )
        cp.start()
        own_copies.append(cp)

    def feed_start(c):
        if not gathered and c < len(cuts):
            for k in range(1, slots):
                feed(c, k).start()

    for c in range(AHEAD):
        feed_start(c)

    buildings = own_ref.shape[1]
    bstep = min(buildings, 1024)
    zmap = map_ref[...]
    row16 = lax.broadcasted_iota(jnp.int32, (16, bstep), 0)

    def find(i, total):
        start = pl.multiple_of(i * bstep, bstep)
        own = own_ref[:, pl.ds(start, bstep)]
        high = own // 128
        digits = jnp.where(row16 == 0, high, jnp.where(row16 == 1, own - high * 128, 0))
        digits = digits.astype(jnp.float32).astype(jnp.bfloat16)
        ids = lax.broadcasted_iota(jnp.int32, (bstep, zones), 0) + start
        hot = (ids == zmap).astype(jnp.float32).astype(jnp.bfloat16)
        return total + jnp.dot(digits, hot, preferred_element_type=jnp.float32)

    found = lax.fori_loop(0, buildings // bstep, find, jnp.zeros((16, zones), jnp.float32))
    owner = found[0:1, :] * 128.0 + found[1:2, :]
    plan[...] = owner.astype(jnp.int32)

    designs = wp_ref.shape[0]
    dstep = min(designs, 64)

    def pick(i, total):
        start = pl.multiple_of(i * dstep, dstep)
        ids = lax.broadcasted_iota(jnp.int32, (dstep, zones), 0) + start
        hot = (ids == plan[...]).astype(jnp.float32).astype(jnp.bfloat16)
        for piece in split3(wp_ref[pl.ds(start, dstep), :]):
            total = total + lax.dot_general(piece, hot, TN, preferred_element_type=jnp.float32)
        return total

    prm[...] = lax.fori_loop(0, designs // dstep, pick, jnp.zeros((width, zones), jnp.float32))

    acc[...] = jnp.zeros_like(acc)
    lane = lax.broadcasted_iota(jnp.int32, (scens, lanes), 1)
    pad_row = lax.broadcasted_iota(jnp.int32, (width, zones), 0)
    hour_first = my_h * hours

    def occupancy(h):
        position = (hour_first + h).astype(jnp.float32)
        return 1.0 + 2.0 * position / (hours_total - 1)

    resp_copy.wait()
    row_tile, zone_tile = min(256, scens), 256

    for c, (first, count) in enumerate(cuts):
        own_copies[c].wait()
        if not gathered:
            for k in range(1, slots):
                feed(c, k).wait_recv()
        feed_start(c + AHEAD)

        def pair_body(j, carry):
            f2 = f_all[j].reshape(scens, lanes)
            ft[j] = f2.astype(jnp.float32).T
            for half in range(2):
                h = 2 * j + half
                coeff = (resp[h].astype(jnp.float32) * prm[...]).astype(jnp.bfloat16)
                mid = 0.25 * (band_ref[pl.ds(h, 1), :].astype(jnp.float32) - 3.5)
                pad = jnp.where(pad_row == 0, -mid, 0.0).astype(jnp.bfloat16)
                if half == 0:
                    left = jnp.where(lane < width, f2.astype(jnp.float32), jnp.where(lane == width, 1.0, 0.0))
                    wcol[half] = jnp.concatenate([coeff, pad], axis=0)
                else:
                    left = jnp.where(lane >= width, f2.astype(jnp.float32), jnp.where(lane == 0, 1.0, 0.0))
                    wcol[half] = jnp.concatenate([pad, coeff], axis=0)
                left = left.astype(jnp.bfloat16)
                weight = floor_ref[...] * occupancy(h)
                for zt in range(zones // zone_tile):
                    zs = slice(zt * zone_tile, (zt + 1) * zone_tile)
                    w_tile = weight[:, zs]
                    for st in range(scens // row_tile):
                        ss = slice(st * row_tile, (st + 1) * row_tile)
                        u = jnp.dot(left[ss, :], wcol[half, :, zs], preferred_element_type=jnp.float32)
                        a = jnp.abs(u) * (-LOG2E)
                        t = jnp.exp2(a)
                        q = t * (t + CROSS) + 1.0
                        cost = (jnp.log2(q) - a) * w_tile
                        part = cost[:, 0:128]
                        for i in range(1, zone_tile // 128):
                            part = part + cost[:, i * 128:(i + 1) * 128]
                        acc[ss, :] += part
                        ub = (u * 0.5).astype(jnp.bfloat16)
                        slope[h, ss, zs] = jnp.tanh(ub - 0.25) + jnp.tanh(ub + 0.25)
            return carry

        lax.fori_loop(first, first + count, pair_body, 0)

    if not gathered:
        for c in range(len(cuts)):
            for k in range(1, slots):
                feed(c, k).wait_send()

    ones = jnp.ones((8, 128), jnp.float32)
    mysum = lax.dot_general(ones, acc[...], NT, precision=HIGH, preferred_element_type=jnp.float32)[0:1, :]
    floor_sum = jnp.sum(floor_ref[...], axis=1, keepdims=True)
    occ_sum = hours + 2.0 / (hours_total - 1) * (
        hours * hour_first.astype(jnp.float32) + hours * (hours - 1) / 2.0
    )
    mw = floor_sum * occ_sum
    mysum = (mysum * LN2) - 0.5 * mw
    slot = my_z * hn + my_h
    sums[my_s, slot] = jnp.concatenate([mysum, jnp.broadcast_to(mw, (1, 128))], axis=1)

    def tell(k):
        return pltpu.make_async_remote_copy(
            src_ref=sums.at[my_s, slot],
            dst_ref=sums.at[my_s, slot],
            send_sem=ssend.at[k],
            recv_sem=srecv.at[k],
            device_id=at(k),
            device_id_type=MESH,
        )

    def heard(k):
        z, s, h = away(k, -1)
        ref = sums.at[s, z * hn + h]
        return pltpu.make_async_remote_copy(
            src_ref=ref, dst_ref=ref, send_sem=ssend.at[k], recv_sem=srecv.at[k],
            device_id=at(k), device_id_type=MESH,
        )

    each_peer(lambda k: tell(k).start())
    each_peer(lambda k: heard(k).wait_recv())

    totals = [jnp.sum(sums[s], axis=0) for s in range(sn)]
    wt = totals[0][:, scens:scens + 1]
    scores = [SHARPNESS * t[:, :scens] / wt for t in totals]
    peak = jnp.max(scores[0], axis=1, keepdims=True)
    for s in scores[1:]:
        peak = jnp.maximum(peak, jnp.max(s, axis=1, keepdims=True))
    exp_total = jnp.sum(jnp.exp(scores[0] - peak), axis=1, keepdims=True)
    for s in scores[1:]:
        exp_total = exp_total + jnp.sum(jnp.exp(s - peak), axis=1, keepdims=True)
    obj_ref[...] = jnp.broadcast_to((peak + jnp.log(exp_total)) / SHARPNESS, obj_ref.shape)
    my_total = jnp.sum(sums[my_s], axis=0)
    sw = jnp.exp(SHARPNESS * my_total[:, :scens] / wt - peak) / exp_total
    each_peer(lambda k: tell(k).wait_send())

    zg[...] = jnp.zeros_like(zg)

    def mix_body(j, carry):
        for half in range(2):
            h = 2 * j + half
            fw = ft[j, half * width:(half + 1) * width, :] * (sw * occupancy(h))
            hi = fw.astype(jnp.bfloat16)
            lo = (fw - hi.astype(jnp.float32)).astype(jnp.bfloat16)
            both = jnp.concatenate([hi, lo], axis=0)
            mixed = jnp.dot(both, slope[h], preferred_element_type=jnp.float32)
            zg[...] += resp[h].astype(jnp.float32) * (mixed[:width] + mixed[width:])
        return carry

    lax.fori_loop(0, hours // 2, mix_body, 0)

    zones_all = zones * zn
    gain = 0.5 * math.sqrt(width * zones_all * hours_total * designs)
    pieces = split3(zg[...] * floor_ref[...] * (gain / wt))
    each = designs // n
    block = 8 * min(n, 16)

    def own_body(i, carry):
        r = lax.broadcasted_iota(jnp.int32, (block, zones), 0) + i * block
        ids = jnp.where(r % 8 < each, (r // 8) * each + r % 8, -1)
        hot = (ids == plan[...]).astype(jnp.float32).astype(jnp.bfloat16)
        total = jnp.zeros((block, width), jnp.float32)
        for piece in pieces:
            total = total + lax.dot_general(hot, piece, NT, preferred_element_type=jnp.float32)
        for b in range(block // 8):
            parts[i * (block // 8) + b] = total[b * 8:(b + 1) * 8, :]
        return carry

    lax.fori_loop(0, n // (block // 8), own_body, 0)

    def give(k):
        z, s, h = away(k)
        return pltpu.make_async_remote_copy(
            src_ref=parts.at[(z * sn + s) * hn + h],
            dst_ref=rbuf.at[k],
            send_sem=rsend.at[k],
            recv_sem=rrecv.at[k],
            device_id=at(k),
            device_id_type=MESH,
        )

    each_peer(lambda k: give(k).start())
    rbuf[0] = parts[me]
    each_peer(lambda k: give(k).wait())
    sens_ref[...] = jnp.sum(rbuf[...], axis=0)[:each, :]


def on_device(forcing, response, window_params, building_map, owner_ids, band_ids, floor_area):
    zn, sn, hn = lax.axis_size("zone"), lax.axis_size("scen"), lax.axis_size("hour")
    n = zn * sn * hn
    hours, width, zones = response.shape
    rows = forcing.shape[0]
    pairs = hours // 2
    gathered = rows % 16 != 0
    if gathered:
        slots, rows_in = 1, rows * zn * hn
        mine = lax.all_to_all(forcing, "hour", split_axis=1, concat_axis=0, tiled=True)
        whole = lax.all_gather(mine, "zone", axis=0, tiled=True)
        fx = whole.reshape(rows_in, pairs, 2 * width).transpose(1, 0, 2)
    else:
        slots, rows_in = zn * hn, rows
        fx = forcing.reshape(rows, hn * pairs, 2 * width).transpose(1, 0, 2)
    chunks = len(chunk_cuts(pairs))
    scens = slots * rows_in
    designs = window_params.shape[0]
    vm = pl.BlockSpec(memory_space=pltpu.VMEM)
    anyspace = pl.BlockSpec(memory_space=pl.ANY)
    dma = pltpu.SemaphoreType.DMA
    f32, bf16 = jnp.float32, jnp.bfloat16
    sens, obj = pl.pallas_call(
        functools.partial(kernel, zn, sn, hn, gathered, hours * hn),
        out_shape=(
            jax.ShapeDtypeStruct((designs // n, width), f32),
            jax.ShapeDtypeStruct((1, 128), f32),
        ),
        in_specs=[anyspace, anyspace, vm, vm, vm, vm, vm],
        out_specs=(vm, vm),
        scratch_shapes=[
            pltpu.VMEM((pairs, slots, rows_in, 2 * width), bf16),
            pltpu.VMEM((hours, width, zones), bf16),
            pltpu.VMEM((pairs, 2 * width, scens), f32),
            pltpu.VMEM((hours, scens, zones), bf16),
            pltpu.VMEM((width, zones), f32),
            pltpu.VMEM((1, zones), jnp.int32),
            pltpu.VMEM((2, 2 * width, zones), bf16),
            pltpu.VMEM((scens, 128), f32),
            pltpu.VMEM((width, zones), f32),
            pltpu.VMEM((sn, zn * hn, 1, scens + 128), f32),
            pltpu.VMEM((n, 8, width), f32),
            pltpu.VMEM((n, 8, width), f32),
            dma,
            dma((chunks,)),
            dma((chunks, slots)),
            dma((chunks, slots)),
            dma((n,)),
            dma((n,)),
            dma((n,)),
            dma((n,)),
        ],
        compiler_params=pltpu.CompilerParams(
            collective_id=0, has_side_effects=True, vmem_limit_bytes=56 * 1024 * 1024
        ),
        cost_estimate=pl.CostEstimate(
            flops=6 * scens * hours * width * zones,
            bytes_accessed=2 * hours * width * zones,
            transcendentals=4 * scens * hours * zones,
        ),
    )(
        fx, response, window_params, building_map.reshape(1, -1), owner_ids.reshape(1, -1),
        band_ids, floor_area.reshape(1, -1),
    )
    return (sens, obj[0, :1])


def solution(mesh):
    in_specs = (
        P(("groups", "zone", "scen", "hour"), None, None),
        P("hour", None, ("groups", "zone")),
        P("groups", None),
        P(("groups", "zone")),
        P("groups"),
        P("hour", ("groups", "zone")),
        P(("groups", "zone")),
    )
    out_specs = (P(("groups", "zone", "scen", "hour"), None), P("groups"))
    return jax.shard_map(
        on_device, mesh=mesh, in_specs=in_specs, out_specs=out_specs, check_vma=False
    )
```
